256 devices in a mesh: vocab: 32 (over y, x, core), rep: 8 (over z).
Axes of the slice: x: 4, y: 4, z: 8, core: 2. Of those that a mesh axis runs over, the one named last changes fastest.
Arguments:
- token_grads: bfloat16 [32768, 16384], P(('vocab', 'rep')), may hold values from -6 to 6
- token_slots: int32 [32768], P(('vocab', 'rep')), may hold values from 0 to 63, as said below
- touched_ids: int32 [16384], P(('vocab', 'rep')), may hold values from 0 to 4095, as said below
- table: float32 [4096, 16384], P('vocab', 'rep'), may hold values from -6 to 6
- first_moment: float32 [4096, 16384], P('vocab', 'rep'), may hold values from -1.75 to 1.75
- second_moment: float32 [4096, 16384], P('vocab', 'rep'), may hold values from 0.01 to 1
Outputs:
- new_table: float32 [4096, 16384], P('vocab', 'rep')
- new_first: float32 [4096, 16384], P('vocab', 'rep')
- new_second: float32 [4096, 16384], P('vocab', 'rep')
- refreshed: bfloat16 [16384, 16384], P(('vocab', 'rep'))
The draws below stay inside these ranges and needn't reach their ends.
Inputs may be any that keep to these rules, and one draw needn't show every extreme that they name: `touched_ids`: each block of 64 entries is strictly ascending. Owner k holds rows k * 128 to (k + 1) * 128 - 1; at most 4 entries of one block fall in one owner's rows, and in every draw one owner receives exactly 4 from every block. `token_slots`: within each block of 128 tokens every position 0 to 63 is named at least once.
All inputs are finite; a program needn't handle non-finite values.
Results may differ from the reference program's by a relative error of at most 0.001.
Values may be sent and summed in bfloat16 or wider, within the bound.
No kernel may reach another device: no remote copies, remote signals or barrier semaphores. Data moves between devices by JAX's collectives and lax.ppermute only.
A program may use at most 128 MiB of HBM per device.

```python
import math
import jax
import jax.numpy as jnp
from jax import lax

D = 16384
ROWS_DEV = 128
TOK_DEV = 128
STEP = 4
UNIQ_DEV = 64
CAP = 4
SENDERS = 256
VOCAB = 4096
TOKENS = 32768


def draw_touched_ids(key, part):
    key = jax.random.fold_in(key, 11)
    owner_total = VOCAB // ROWS_DEV
    hot_owner = jax.random.randint(jax.random.fold_in(key, 1), (), 0, owner_total)
    owner_index = jnp.arange(owner_total, dtype=jnp.int32)[:, None]

    def one_block(device_key):
        key_rows, key_pick = jax.random.split(device_key)

        def owner_rows(row_key):
            return jnp.sort(jax.random.permutation(row_key, ROWS_DEV)[:CAP])
        candidates = jax.vmap(owner_rows)(jax.random.split(key_rows, owner_total))
        row_ids = (owner_index * ROWS_DEV + candidates).reshape(-1)
        priority = jax.random.permutation(key_pick, owner_total * CAP).reshape(owner_total, CAP)
        priority = jnp.where(owner_index == hot_owner, -1, priority).reshape(-1)
        ranked = jnp.argsort(priority, stable=True)
        chosen = jnp.sort(ranked[:UNIQ_DEV])
        return jnp.take(row_ids, chosen, axis=0)
    device_keys = jax.random.split(jax.random.fold_in(key, 2), SENDERS)
    return jax.vmap(one_block)(device_keys).reshape(-1).astype(jnp.int32)


def draw_token_slots(key, part):
    key = jax.random.fold_in(key, 12)

    def one_block(device_key):
        key_base, key_left, key_right, key_mix = jax.random.split(device_key, 4)
        base = jax.random.permutation(key_base, UNIQ_DEV)
        extra_left = jax.random.randint(key_left, (TOK_DEV - UNIQ_DEV,), 0, UNIQ_DEV)
        extra_right = jax.random.randint(key_right, (TOK_DEV - UNIQ_DEV,), 0, UNIQ_DEV)
        joined = jnp.concatenate([base, jnp.minimum(extra_left, extra_right)])
        return jnp.take(joined, jax.random.permutation(key_mix, TOK_DEV), axis=0)
    return jax.vmap(one_block)(jax.random.split(key, SENDERS)).reshape(-1).astype(jnp.int32)


def level_of(own_key, shape, cuts, least, top_value):
    def one(dim, shards_of):
        heights = jax.random.uniform(jax.random.fold_in(jax.random.fold_in(own_key, 6), dim), (shards_of,), jnp.float32, least / len(cuts), top_value / len(cuts))
        return jnp.repeat(jnp.exp(heights), shape[dim] // shards_of).reshape((-1,) + (1,) * (len(shape) - dim - 1))

    gain = one(*cuts[0])
    for cut in cuts[1:]:
        gain = gain * one(*cut)
    return gain


def scatter_about(stream_key, shape, scale, most, cuts=(), kind=jnp.bfloat16):
    drawn = scale * jax.random.normal(stream_key, shape, jnp.float32)
    if cuts:
        drawn = drawn * level_of(stream_key, shape, cuts, -0.22, 0.18)
    return jnp.clip(drawn, -most, most).astype(kind)


def setup_inputs(seed: int = 0) -> dict:
    keys = jax.random.split(jax.random.key(seed), 7)
    return {
        "token_grads": scatter_about(keys[0], (TOKENS, D), 1.0, 6.0, ((0, 256),)),
        "token_slots": draw_token_slots(jax.random.fold_in(keys[6], 71), 0),
        "touched_ids": draw_touched_ids(jax.random.fold_in(keys[6], 71), 0),
        "table": scatter_about(keys[3], (VOCAB, D), 1.0, 6.0, ((0, 32), (1, 8)), jnp.float32),
        "first_moment": scatter_about(keys[4], (VOCAB, D), 0.3, 1.75, ((0, 32), (1, 8)), jnp.float32),
        "second_moment": jnp.clip(jnp.exp(math.log(1.0) - 4.6051702 * jax.random.uniform(keys[5], (VOCAB, D), jnp.float32) ** level_of(keys[5], (VOCAB, D), ((0, 32), (1, 8)), -0.2, 0.2)), 0.01, 1.0),
    }


decay_first = 0.9
decay_second = 0.95
learn_rate = 0.03
epsilon = 1e-08

def adam_step(table, first_moment, second_moment, gradient):
    new_first = decay_first * first_moment + (1.0 - decay_first) * gradient
    new_second = decay_second * second_moment + (1.0 - decay_second) * gradient * gradient
    scaled_first = new_first / (1.0 - decay_first ** STEP)
    scaled_second = new_second / (1.0 - decay_second ** STEP)
    new_table = table - learn_rate * scaled_first / (jnp.sqrt(scaled_second) + epsilon)
    return (new_table, new_first, new_second)

def reference(token_grads, token_slots, touched_ids, table, first_moment, second_moment):
    grad_blocks = token_grads.reshape(SENDERS, TOK_DEV, D)
    slot_blocks = token_slots.reshape(SENDERS, TOK_DEV)
    id_blocks = touched_ids.reshape(SENDERS, UNIQ_DEV)

    def add_block(gradient, block):
        grads_here, slots_here, ids_here = block
        row_of = jnp.take(ids_here, slots_here.astype(jnp.int32), axis=0).astype(jnp.int32)
        return (gradient.at[row_of].add(grads_here.astype(jnp.float32)), None)
    gradient, _ = lax.scan(add_block, jnp.zeros((VOCAB, D), jnp.float32), (grad_blocks, slot_blocks, id_blocks))
    new_table, new_first, new_second = adam_step(table, first_moment, second_moment, gradient)
    refreshed = jnp.take(new_table, touched_ids.astype(jnp.int32), axis=0).astype(jnp.bfloat16)
    return (new_table, new_first, new_second, refreshed)
```

```python
import functools
import jax
import jax.numpy as jnp
from jax import lax
from jax.experimental import pallas as pl
from jax.experimental.pallas import tpu as pltpu
from jax.sharding import PartitionSpec as P

STEP = 4
decay_first = 0.9
decay_second = 0.95
learn_rate = 0.03
epsilon = 1e-08

CAP = 4
STEP_COLUMNS = 256
SUB, LANES = 8, 128
f32, bf16, i32 = jnp.float32, jnp.bfloat16, jnp.int32
sds = jax.ShapeDtypeStruct
ANY = pl.BlockSpec(memory_space=pl.ANY)


def iota(shape, dim):
    return lax.broadcasted_iota(i32, shape, dim)


def ones(hit):
    return jnp.where(hit, 1.0, 0.0).astype(bf16)


def whole(shape):
    return pl.BlockSpec(shape, lambda *_: (0,) * len(shape))


def call(body, name, out_shape, grid, in_specs, out_specs, flops, nbytes, aliases=None, scratch=()):
    return pl.pallas_call(
        body,
        out_shape=out_shape,
        grid_spec=pltpu.PrefetchScalarGridSpec(
            num_scalar_prefetch=1,
            grid=grid,
            in_specs=in_specs,
            out_specs=out_specs,
            scratch_shapes=scratch,
        ),
        input_output_aliases=aliases or {},
        compiler_params=pltpu.CompilerParams(vmem_limit_bytes=32 << 20),
        cost_estimate=pl.CostEstimate(flops=flops, bytes_accessed=nbytes, transcendentals=0),
        name=name,
    )


def parts_dot(onehot, values, contract):
    total = None
    for step in range(3):
        part = values.astype(bf16)
        if step < 2:
            values = values - part.astype(f32)
        term = lax.dot_general(onehot, part, ((contract, (0,)), ((), ())), preferred_element_type=f32)
        total = term if total is None else total + term
    return total


def positions(ids_row, owned):
    n = ids_row.shape[1]
    ids = jnp.broadcast_to(ids_row, (n, n))
    at, along = iota((n, n), 0), iota((n, n), 1)
    owner_row = ids // owned
    ids_col = jnp.sum(jnp.where(at == along, ids, 0), axis=1, keepdims=True)
    owner_col = jnp.broadcast_to(ids_col // owned, (n, n))
    same = owner_row == owner_col
    rank_row = jnp.sum(jnp.where(same & (at < along), 1, 0), axis=0, keepdims=True)
    rank_col = jnp.sum(jnp.where(same & (along < at), 1, 0), axis=1, keepdims=True)
    return owner_row[:1] * CAP + rank_row, owner_col[:, :1] * CAP + rank_col


def sums_kernel(reps, me_ref, slots_ref, ids_ref, *refs):
    ins, outs = refs[:reps], refs[reps:]
    n, tokens = ids_ref.shape[1], slots_ref.shape[1]
    wa = ins[0].shape[1]
    member = ones(jnp.broadcast_to(slots_ref[...], (n, tokens)) == iota((n, tokens), 0))
    names = jnp.broadcast_to(ids_ref[...], (SUB, n)).astype(f32)
    for i, o in zip(ins, outs):
        total = jnp.dot(member, i[...], preferred_element_type=f32)
        for g in range(n // SUB):
            o[:, g * wa : (g + 1) * wa] = total[g * SUB : (g + 1) * SUB]
        o[:, n // SUB * wa : n // SUB * wa + LANES] = jnp.zeros((SUB, LANES), f32)
        o[:, n // SUB * wa : n // SUB * wa + n] = names


def tags_of(row_at, ids_row, places_row, owned):
    hit = row_at == places_row
    return jnp.sum(jnp.where(hit, ids_row % owned + 1, 0), axis=1, keepdims=True) - 1


def send_kernel(owned, me_ref, slots_ref, ids_ref, *refs):
    ins, (out_ref, buf, sems) = refs[:-3], refs[-3:]
    half, wb = len(ins) // 2, ins[0].shape[1]
    rows, tokens, n = buf.shape[0], slots_ref.shape[1], ids_ref.shape[1]
    place_row, place_col = positions(ids_ref[...], owned)
    slot = jnp.broadcast_to(slots_ref[...], (n, tokens))
    of_token = jnp.sum(
        jnp.where(slot == iota((n, tokens), 0), place_col, 0), axis=0, keepdims=True
    )
    row = iota((rows, tokens), 0)
    hit = (row // (2 * CAP) * CAP + row % CAP) == of_token
    upper = row // CAP % 2
    member = [ones(hit & (upper == h)) for h in range(2)]
    row = iota((rows, n), 0)
    tag = tags_of(row // (2 * CAP) * CAP + row % CAP, ids_ref[...], place_row, owned)
    copies = []
    for i in range(half + 1):
        at = pl.ds(i * wb, wb if i < half else LANES)
        if i < half:
            buf[:, at] = jnp.dot(member[0], ins[i][...], preferred_element_type=f32) + jnp.dot(
                member[1], ins[half + i][...], preferred_element_type=f32
            )
        else:
            buf[:, at] = jnp.broadcast_to(tag, (rows, LANES)).astype(f32)
        copies.append(pltpu.make_async_copy(buf.at[:, at], out_ref.at[:, at], sems.at[i]))
        copies[-1].start()
    for copy in copies:
        copy.wait()


def route_kernel(owned, wa, me_ref, *refs):
    ins, (out_ref, buf, sems) = refs[:-3], refs[-3:]
    owners = buf.shape[0]
    n = (ins[0].shape[1] - LANES) // wa * SUB
    pairs = len(ins) // 2
    rows = owners * 2 * CAP
    tags = jnp.zeros((rows, LANES), i32)
    copies = []
    for pair in range(pairs):
        hits, blocks, tag = [], [], 0
        for t in range(2):
            x = ins[2 * pair + t]
            ids_row = x[:1, n // SUB * wa : n // SUB * wa + n].astype(i32)
            place_row, _ = positions(ids_row, owned)
            at = iota((rows, n), 0)
            here = jnp.where(at // CAP % 2 == t, at // (2 * CAP) * CAP + at % CAP, -1)
            hits.append(ones(here == place_row))
            tag = tag + tags_of(here, ids_row, place_row, owned) + 1
            blocks.append(x)
        tags = jnp.where(iota((rows, LANES), 1) == pair, tag - 1, tags)
        onehot = jnp.concatenate(hits, axis=1)
        for c in range(wa // STEP_COLUMNS):
            values = jnp.concatenate(
                [
                    x[:, g * wa + c * STEP_COLUMNS : g * wa + (c + 1) * STEP_COLUMNS]
                    for x in blocks
                    for g in range(n // SUB)
                ],
                axis=0,
            )
            start = pair * wa + c * STEP_COLUMNS
            buf[:, :, start : start + STEP_COLUMNS] = parts_dot(onehot, values, (1,)).reshape(
                owners, 2 * CAP, STEP_COLUMNS
            )
        at = pl.ds(pair * wa, wa)
        copies.append(pltpu.make_async_copy(buf.at[:, :, at], out_ref.at[:, :, at], sems.at[pair]))
        copies[-1].start()
    at = pl.ds(pairs * wa, LANES)
    buf[:, :, at] = tags.astype(f32).reshape(owners, 2 * CAP, LANES)
    copies.append(pltpu.make_async_copy(buf.at[:, :, at], out_ref.at[:, :, at], sems.at[pairs]))
    copies[-1].start()
    for copy in copies:
        copy.wait()


def place_kernel(owned, me_ref, tags_ref, in_ref, out_ref, placer):
    rows = in_ref.shape[0]

    @pl.when((pl.program_id(0) == 0) & (pl.program_id(1) == 0))
    def _():
        shape = (rows, owned)
        hit = tags_ref[...][:, :1].astype(i32) == iota(shape, 1)
        upper = iota(shape, 0) // CAP % 2
        for h in range(2):
            placer[:, h * owned : (h + 1) * owned] = ones(hit & (upper == h))

    out_ref[...] = parts_dot(placer[...], in_ref[...], (0,)).reshape(out_ref.shape)


def step(gradient, table_ref, first_ref, second_ref, new_table_ref, new_first_ref, new_second_ref):
    new_first = decay_first * first_ref[...] + (1.0 - decay_first) * gradient
    new_second = decay_second * second_ref[...] + (1.0 - decay_second) * gradient * gradient
    scaled_first = new_first / (1.0 - decay_first**STEP)
    scaled_second = new_second / (1.0 - decay_second**STEP)
    new_table = table_ref[...] - learn_rate * scaled_first / (jnp.sqrt(scaled_second) + epsilon)
    new_table_ref[...] = new_table
    new_first_ref[...] = new_first
    new_second_ref[...] = new_second
    return new_table.astype(bf16)


def adam_a_kernel(pairs, me_ref, tags_ref, *refs):
    ins, out_ref, hits = refs[:pairs], refs[-2], refs[-1]
    rows, owned = hits.shape

    @pl.when(pl.program_id(0) == 0)
    def _():
        tags = tags_ref[...]
        tag = jnp.concatenate([tags[:, :, j : j + 1] for j in range(pairs)], axis=1).reshape(rows, 1)
        hits[...] = ones(tag.astype(i32) == iota((rows, owned), 1))

    values = jnp.concatenate([x[...] for x in ins], axis=1).reshape(rows, -1)
    half = step(parts_dot(hits[...], values, (0,)), *refs[pairs:-2])
    out_ref[...] = (
        jnp.dot(hits[...], half, preferred_element_type=f32).astype(bf16).reshape(out_ref.shape)
    )


def adam_b_kernel(me_ref, grad_ref, *refs):
    refs[-1][...] = step(grad_ref[...], *refs[:3], *refs[-4:-1])


def pick_kernel(owned, me_ref, tags_ref, in_ref, out_ref, picker):
    rows = out_ref.shape[0]

    @pl.when((pl.program_id(0) == 0) & (pl.program_id(1) == 0))
    def _():
        tags = tags_ref[...].reshape(rows // (4 * CAP), 2 * CAP, LANES)
        tags = jnp.concatenate([tags, tags], axis=1).reshape(rows, LANES)
        shape = (rows, owned)
        hit = tags[:, :1].astype(i32) == iota(shape, 1)
        quarter = iota(shape, 0) // CAP % 4
        for h in range(4):
            picker[:, h * owned : (h + 1) * owned] = ones(hit & (quarter == h))

    block = in_ref[...].reshape(4 * owned, in_ref.shape[-1])
    out_ref[...] = jnp.dot(picker[...], block, preferred_element_type=f32).astype(bf16)


def unpad_kernel(owned, reps, me_ref, in_ref, *refs):
    names, outs = refs[:reps], refs[reps:]
    owners = in_ref.shape[0]
    n = outs[0].shape[0]
    for group in range(reps // 4):
        block = in_ref[:, group * 4 * CAP : (group + 1) * 4 * CAP, :].reshape(owners * 4 * CAP, -1)
        for t in range(4):
            s = 4 * group + t
            _, col = positions(names[s][:1, :n].astype(i32), owned)
            at = iota((n, owners * 4 * CAP), 1)
            hit = ((at // (4 * CAP) * CAP + at % CAP) == col) & (at // CAP % 4 == t)
            outs[s][...] = jnp.dot(ones(hit), block, preferred_element_type=f32).astype(bf16)


def final_kernel(owned, reps, width, wa, me_ref, ids_ref, in_ref, *refs):
    ins, out_ref, found, sems, sem_b = refs[:reps], refs[-4], refs[-3], refs[-2], refs[-1]
    r = me_ref[1]
    n = out_ref.shape[0]
    copies = []
    for s in range(reps):
        start = pl.multiple_of((r + s) % reps * width, 128)
        copies.append(pltpu.make_async_copy(ins[s], out_ref.at[:, pl.ds(start, wa)], sems.at[s]))
        copies[-1].start()
    _, col = positions(ids_ref[...], owned)
    wb = width - wa
    rows = in_ref.shape[0]
    at = iota((n, rows), 1)
    hit = (at // (4 * CAP) * CAP + at % CAP) == col
    for h in range(4):
        onehot = ones(hit & (at // CAP % 4 == h))
        for i in range(2):
            q = 2 * h + i
            found[q] = jnp.dot(
                onehot, in_ref[:, i * wb : (i + 1) * wb], preferred_element_type=f32
            ).astype(bf16)
            copies.append(
                pltpu.make_async_copy(found.at[q], out_ref.at[:, pl.ds(q * width + wa, wb)], sem_b.at[q])
            )
            copies[-1].start()
    for copy in copies:
        copy.wait()


def shards(token_grads, token_slots, touched_ids, table, first_moment, second_moment):
    owners, reps = lax.axis_size("vocab"), lax.axis_size("rep")
    tokens, full = token_grads.shape
    touched = touched_ids.shape[0]
    owned, width = table.shape
    wa = width // 2
    wb = width - wa
    cols = STEP_COLUMNS
    half = reps // 2
    rows8, rows16, rows_all = owners * 2 * CAP, owners * 4 * CAP, owners * reps * CAP
    slots = token_slots.reshape(1, tokens)
    ids = touched_ids.reshape(1, touched)
    me = jnp.stack([lax.axis_index("vocab"), lax.axis_index("rep")]).astype(i32)

    def over_vocab(x):
        return lax.all_to_all(x, "vocab", split_axis=0, concat_axis=0, tiled=True)

    def shift(x, s):
        if s == 0:
            return x
        return lax.ppermute(x, "rep", [(i, (i + s) % reps) for i in range(reps)])

    wide_a = touched // SUB * wa + LANES
    sums = call(
        functools.partial(sums_kernel, reps),
        "sums",
        [sds((SUB, wide_a), f32)] * reps,
        (1,),
        [whole((1, tokens)), whole((1, touched))]
        + [
            pl.BlockSpec((tokens, wa), lambda i, me, s=s: (0, (me[1] + s) % reps * (width // wa)))
            for s in range(reps)
        ],
        [whole((SUB, wide_a))] * reps,
        2 * touched * tokens * wa * reps,
        (tokens * 2 + touched * 4) * wa * reps,
    )(me, slots, ids, *[token_grads] * reps)
    group = [shift(x, s) for s, x in enumerate(sums)]

    per = wb // cols
    wide_b = half * wb + LANES
    out_b = call(
        functools.partial(send_kernel, owned),
        "send",
        sds((rows8, wide_b), f32),
        (1,),
        [whole((1, tokens)), whole((1, touched))]
        + [pl.BlockSpec((tokens, wb), lambda i, me, q=q: (0, (q * width + wa) // wb)) for q in range(reps)],
        ANY,
        4 * rows8 * tokens * wb * half,
        (tokens * 4 + rows8 * 4) * wb * half,
        scratch=[pltpu.VMEM((rows8, wide_b), f32), pltpu.SemaphoreType.DMA((half + 1,))],
    )(me, slots, ids, *[token_grads] * reps)
    arrived_b = over_vocab(out_b.reshape(owners, 2 * CAP, -1)).reshape(rows8, -1)
    arrived_b, *group = lax.optimization_barrier((arrived_b, *group))
    tags_b = pl.BlockSpec((rows8, LANES), lambda i, j, me: (0, half * wb // LANES))

    dense = call(
        functools.partial(place_kernel, owned),
        "place",
        sds((2, half, owned, wb), f32),
        (half, per),
        [tags_b, pl.BlockSpec((rows8, cols), lambda i, j, me: (0, i * per + j))],
        pl.BlockSpec((2, 1, owned, cols), lambda i, j, me: (0, i, 0, j)),
        6 * rows8 * 2 * owned * wb * half,
        2 * rows8 * half * wb * 4,
        scratch=[pltpu.VMEM((rows8, 2 * owned), bf16)],
    )(me, arrived_b, arrived_b)
    gradient_b = lax.psum_scatter(
        dense.reshape(reps * owned, wb), "rep", scatter_dimension=0, tiled=True
    )

    steps_a = wa // cols
    wide = half * wa + LANES
    out_a = call(
        functools.partial(route_kernel, owned, wa),
        "route",
        sds((owners, 2 * CAP, wide), f32),
        (1,),
        [whole((SUB, wide_a))] * reps,
        ANY,
        6 * rows_all * 2 * touched * wa,
        (rows_all + reps * touched) * 4 * wa,
        scratch=[pltpu.VMEM((owners, 2 * CAP, wide), f32), pltpu.SemaphoreType.DMA((half + 1,))],
    )(me, *group)
    arrived_a = over_vocab(out_a)

    spec = pl.BlockSpec((owned, cols), lambda i, me: (0, i))
    *news, back_a = call(
        functools.partial(adam_a_kernel, half),
        "adam_a",
        [*(sds((owned, width), f32) for _ in range(3)), sds((owners, reps * CAP, wa), bf16)],
        (steps_a,),
        [pl.BlockSpec((owners, 2 * CAP, LANES), lambda i, me: (0, 0, half * wa // LANES))]
        + [
            pl.BlockSpec((owners, 2 * CAP, cols), lambda i, me, j=j: (0, 0, j * steps_a + i))
            for j in range(half)
        ]
        + [spec, spec, spec],
        [spec, spec, spec, pl.BlockSpec((owners, reps * CAP, cols), lambda i, me: (0, 0, i))],
        8 * rows_all * owned * wa,
        (rows_all * 6 + owned * 24) * wa,
        scratch=[pltpu.VMEM((rows_all, owned), bf16)],
    )(me, *[arrived_a] * (half + 1), table, first_moment, second_moment)
    returned_a = over_vocab(back_a)

    spec_b = pl.BlockSpec((owned, cols), lambda i, me: (0, wa // cols + i))
    spec_g = pl.BlockSpec((owned, cols), lambda i, me: (0, i))
    *news, half_b = call(
        adam_b_kernel,
        "adam_b",
        [*(sds((owned, width), f32) for _ in range(3)), sds((owned, wb), bf16)],
        (per,),
        [spec_g, spec_b, spec_b, spec_b, ANY, ANY, ANY],
        [spec_b, spec_b, spec_b, spec_g],
        20 * owned * wb,
        30 * owned * wb,
        aliases={5: 0, 6: 1, 7: 2},
    )(me, gradient_b, table, first_moment, second_moment, *news)
    rows_b = lax.all_gather(half_b, "rep", axis=0, tiled=True)

    mine_a = call(
        functools.partial(unpad_kernel, owned, reps),
        "unpad",
        [sds((touched, wa), bf16)] * reps,
        (steps_a,),
        [pl.BlockSpec((owners, reps * CAP, cols), lambda i, me: (0, 0, i))]
        + [pl.BlockSpec((SUB, LANES), lambda i, me: (0, touched // SUB * wa // LANES))] * reps,
        [pl.BlockSpec((touched, cols), lambda i, me: (0, i))] * reps,
        2 * reps * touched * rows16 * wa,
        (rows_all + reps * touched) * 2 * wa,
    )(me, returned_a, *group)
    home_a = [shift(x, (reps - s) % reps) for s, x in enumerate(mine_a)]

    back_b = call(
        functools.partial(pick_kernel, owned),
        "pick",
        sds((rows16, 2 * wb), bf16),
        (2, per),
        [
            tags_b,
            pl.BlockSpec((4, 1, owned, cols), lambda i, j, me: (0, i, 0, j)),
        ],
        pl.BlockSpec((rows16, cols), lambda i, j, me: (0, i * per + j)),
        4 * rows16 * 4 * owned * wb,
        (8 * owned + 2 * rows16) * wb * 2,
        scratch=[pltpu.VMEM((rows16, 4 * owned), bf16)],
    )(me, arrived_b, rows_b.reshape(4, 2, owned, wb))
    returned_b = over_vocab(back_b.reshape(owners, 4 * CAP, -1)).reshape(rows16, -1)

    refreshed = call(
        functools.partial(final_kernel, owned, reps, width, wa),
        "final",
        sds((touched, full), bf16),
        (1,),
        [whole((1, touched)), whole((rows16, 2 * wb))] + [ANY] * reps,
        ANY,
        16 * touched * rows16 * wb,
        touched * full * 4,
        scratch=[
            pltpu.VMEM((reps, touched, wb), bf16),
            pltpu.SemaphoreType.DMA((reps,)),
            pltpu.SemaphoreType.DMA((reps,)),
        ],
    )(me, ids, returned_b, *home_a)
    return (*news, refreshed)


def solution(mesh):
    return jax.shard_map(
        shards,
        mesh=mesh,
        in_specs=(
            P(("vocab", "rep"), None),
            P(("vocab", "rep")),
            P(("vocab", "rep")),
            P("vocab", "rep"),
            P("vocab", "rep"),
            P("vocab", "rep"),
        ),
        out_specs=(
            P("vocab", "rep"),
            P("vocab", "rep"),
            P("vocab", "rep"),
            P(("vocab", "rep"), None),
        ),
        check_vma=False,
    )
```

```python
import functools
import math
import jax
import jax.numpy as jnp
from jax import lax
from jax.experimental import pallas as pl
from jax.experimental.pallas import tpu as pltpu
from jax.sharding import PartitionSpec as P

STEP = 4
decay_first = 0.9
decay_second = 0.95
learn_rate = 0.03
epsilon = 1e-08

CAP = 4
QUAD = 4
SUB, LANES = 16, 128
PART_A, COLS, COLS_B = 1152, 384, 128
SOON = (1, 7)
TOP = 32000.0
PER_OCTAVE = 64.0 / math.log(2.0)
f32, bf16, i32, i16 = jnp.float32, jnp.bfloat16, jnp.int32, jnp.int16
sds = jax.ShapeDtypeStruct
ANY = pl.BlockSpec(memory_space=pl.ANY)


def iota(shape, dim):
    return lax.broadcasted_iota(i32, shape, dim)


def ones(hit):
    return jnp.where(hit, 1.0, 0.0).astype(bf16)


def whole(shape):
    return pl.BlockSpec(shape, lambda *_: (0,) * len(shape))


def call(body, name, out_shape, grid, in_specs, out_specs, flops, nbytes, aliases=None, scratch=(), room=24):
    return pl.pallas_call(
        body,
        out_shape=out_shape,
        grid_spec=pltpu.PrefetchScalarGridSpec(
            num_scalar_prefetch=1,
            grid=grid,
            in_specs=in_specs,
            out_specs=out_specs,
            scratch_shapes=scratch,
        ),
        input_output_aliases=aliases or {},
        compiler_params=pltpu.CompilerParams(vmem_limit_bytes=room << 20),
        cost_estimate=pl.CostEstimate(flops=flops, bytes_accessed=nbytes, transcendentals=0),
        name=name,
    )


def to_i16(values):
    return values.astype(i32).astype(i16)


def to_f32(codes):
    return codes.astype(i32).astype(f32)


def encode(values):
    most = jnp.max(jnp.abs(values), axis=1, keepdims=True)
    level = jnp.ceil(jnp.log(jnp.maximum(most, 1e-30)) * PER_OCTAVE)
    return to_i16(jnp.round(values * (jnp.exp(level * (-1.0 / PER_OCTAVE)) * TOP))), level


def decode(codes, level):
    return to_f32(codes) * (jnp.exp(to_f32(level) * (1.0 / PER_OCTAVE)) * (1.0 / TOP))


def halves_dot(onehot, values):
    upper = values.astype(bf16)
    lower = (values - upper.astype(f32)).astype(bf16)
    return jnp.dot(onehot, upper, preferred_element_type=f32) + jnp.dot(
        onehot, lower, preferred_element_type=f32
    )


def codes_dot(onehot, codes):
    upper = jnp.floor(codes * (1.0 / 256.0))
    lower = codes - upper * 256.0
    return 256.0 * jnp.dot(onehot, upper.astype(bf16), preferred_element_type=f32) + jnp.dot(
        onehot, lower.astype(bf16), preferred_element_type=f32
    )


def positions(ids_row, owned):
    n = ids_row.shape[1]
    ids = jnp.broadcast_to(ids_row, (n, n))
    at, along = iota((n, n), 0), iota((n, n), 1)
    owner_row = ids // owned
    ids_col = jnp.sum(jnp.where(at == along, ids, 0), axis=1, keepdims=True)
    owner_col = jnp.broadcast_to(ids_col // owned, (n, n))
    same = owner_row == owner_col
    rank_row = jnp.sum(jnp.where(same & (at < along), 1, 0), axis=0, keepdims=True)
    rank_col = jnp.sum(jnp.where(same & (along < at), 1, 0), axis=1, keepdims=True)
    return owner_row[:1] * CAP + rank_row, owner_col[:, :1] * CAP + rank_col, ids_col


def place_of(at):
    return at // (QUAD * CAP) * CAP + at % CAP


def which(at):
    return at // CAP % QUAD


def load_columns(source, buf, sems, firsts):
    width = buf.shape[2]
    copies = [
        pltpu.make_async_copy(source.at[:, pl.ds(first, width)], buf.at[j], sems.at[j])
        for j, first in enumerate(firsts)
    ]
    for copy in copies:
        copy.start()
    return copies


def sums_kernel(width, me_ref, slots_ref, ids_ref, grads_ref, *refs):
    outs, (buf, sems) = refs[:-2], refs[-2:]
    reps, n, tokens, wa = len(outs), ids_ref.shape[1], slots_ref.shape[1], buf.shape[2]
    copies = load_columns(
        grads_ref,
        buf,
        sems,
        [pl.multiple_of((me_ref[1] + s) % reps * width, LANES) for s in range(reps)],
    )
    member = ones(jnp.broadcast_to(slots_ref[...], (n, tokens)) == iota((n, tokens), 0))
    lane = iota((SUB, LANES), 1)
    names = jnp.concatenate([jnp.broadcast_to(ids_ref[...], (SUB, n)), jnp.zeros((SUB, LANES - n), i32)], axis=1)
    for s in range(reps):
        copies[s].wait()
        codes, level = encode(jnp.dot(member, buf[s], preferred_element_type=f32))
        tile = names.astype(f32)
        for g in range(n // SUB):
            outs[s][:, g * wa : (g + 1) * wa] = codes[g * SUB : (g + 1) * SUB]
            tile = jnp.where(lane == n + g, level[g * SUB : (g + 1) * SUB], tile)
        outs[s][:, n // SUB * wa :] = to_i16(tile)


def send_kernel(width, wa, owned, me_ref, slots_ref, ids_ref, after_ref, grads_ref, out_ref, buf, made, sems, out_sems):
    reps, tokens, wb = buf.shape
    n, rows = ids_ref.shape[1], made.shape[0]
    copies = load_columns(
        grads_ref,
        buf,
        sems,
        [s * width + wa for s in range(reps)],
    )
    place_row, place_col, _ = positions(ids_ref[...], owned)
    slot = jnp.broadcast_to(slots_ref[...], (n, tokens))
    of_token = jnp.sum(
        jnp.where(slot == iota((n, tokens), 0), place_col, 0), axis=0, keepdims=True
    )
    at = iota((rows, tokens), 0)
    hit = place_of(at) == of_token
    member = jnp.concatenate([ones(hit & (which(at) == h)) for h in range(QUAD)], axis=1)
    local = ids_ref[...] % owned + 1
    held = jnp.sum(jnp.where(place_of(iota((rows, n), 0)) == place_row, local, 0), axis=1, keepdims=True)
    lane = iota((rows, LANES), 1)
    tile = jnp.where(lane == 2, held, 0).astype(f32)
    for copy in copies:
        copy.wait()
    sent = []
    for i in range(3):
        if i < 2:
            block = jnp.concatenate([buf[2 * h + i] for h in range(QUAD)], axis=0)
            codes, level = encode(jnp.dot(member, block, preferred_element_type=f32))
            tile = jnp.where(lane == i, level, tile)
            cut = pl.ds(i * wb, wb)
            made[:, cut] = codes
        else:
            cut = pl.ds(2 * wb, LANES)
            made[:, cut] = to_i16(tile)
        sent.append(pltpu.make_async_copy(made.at[:, cut], out_ref.at[:, cut], out_sems.at[i]))
        sent[-1].start()
    for copy in sent:
        copy.wait()


def route_kernel(owned, wa, me_ref, *refs):
    ins, (out_ref, made, sems) = refs[:-3], refs[-3:]
    rows = made.shape[0]
    groups = (ins[0].shape[1] - LANES) // wa
    n = groups * SUB
    lane = iota((rows, LANES), 1)
    tile = jnp.zeros((rows, LANES), f32)
    hits = []
    for j in range(len(ins) // QUAD):
        hot, extra = [], []
        for t in range(QUAD):
            last = ins[QUAD * j + t][:, groups * wa :].astype(i32)
            place_row, _, ids_col = positions(last[:1, :n], owned)
            at = iota((rows, n), 0)
            hot.append(ones((place_of(at) == place_row) & (which(at) == t)))
            level = jnp.concatenate([last[:, n + g : n + g + 1] for g in range(groups)], axis=0)
            pair = iota((n, LANES), 1)
            extra.append(
                jnp.where(pair == 2 * j, level, jnp.where(pair == 2 * j + 1, ids_col % owned + 1, 0)).astype(f32)
            )
        hits.append(jnp.concatenate(hot, axis=1))
        tile = tile + codes_dot(hits[j], jnp.concatenate(extra, axis=0))
    made[:, 2 * wa :] = to_i16(tile)
    sent = [pltpu.make_async_copy(made.at[:, pl.ds(2 * wa, LANES)], out_ref.at[:, pl.ds(2 * wa, LANES)], sems.at[0])]
    sent[-1].start()
    for c in range(wa // COLS):
        for j in range(len(hits)):
            codes = jnp.concatenate(
                [
                    to_f32(x[:, g * wa + c * COLS : g * wa + (c + 1) * COLS])
                    for x in ins[QUAD * j : QUAD * (j + 1)]
                    for g in range(groups)
                ],
                axis=0,
            )
            first = (2 * c + j) * COLS
            made[:, first : first + COLS] = to_i16(codes_dot(hits[j], codes))
        cut = pl.ds(2 * c * COLS, 2 * COLS)
        sent.append(pltpu.make_async_copy(made.at[:, cut], out_ref.at[:, cut], sems.at[c + 1]))
        sent[-1].start()
    for copy in sent:
        copy.wait()


def place_kernel(owned, wb, me_ref, in_ref, out_ref, made, sems):
    rows = in_ref.shape[0]
    tile = in_ref[:, 2 * wb :]
    held = tile[:, 2:3].astype(i32)
    shape = (rows, owned)
    hit = jnp.where(held == iota(shape, 1) + 1, 1.0, 0.0).T
    quarter = which(iota((owned, rows), 1))
    placer = jnp.concatenate(
        [jnp.where(quarter == h, hit, 0.0).astype(bf16) for h in range(QUAD)], axis=0
    )
    sent = []
    for i in range(2):
        values = decode(in_ref[:, i * wb : (i + 1) * wb], tile[:, i : i + 1])
        made[i] = halves_dot(placer, values)
        for h in range(QUAD):
            q = 2 * h + i
            sent.append(
                pltpu.make_async_copy(
                    made.at[i, pl.ds(h * owned, owned)], out_ref.at[pl.ds(q * owned, owned)], sems.at[q]
                )
            )
            sent[-1].start()
    for copy in sent:
        copy.wait()


def step(gradient, table_ref, first_ref, second_ref, new_table_ref, new_first_ref, new_second_ref):
    new_first = decay_first * first_ref[...] + (1.0 - decay_first) * gradient
    new_second = decay_second * second_ref[...] + (1.0 - decay_second) * gradient * gradient
    scaled_first = new_first / (1.0 - decay_first**STEP)
    scaled_second = new_second / (1.0 - decay_second**STEP)
    new_table = table_ref[...] - learn_rate * scaled_first / (jnp.sqrt(scaled_second) + epsilon)
    new_table_ref[...] = new_table
    new_first_ref[...] = new_first
    new_second_ref[...] = new_second
    return new_table.astype(bf16)


def adam_a_kernel(me_ref, tile_ref, in_ref, *refs):
    out_ref, hits, turned = refs[-3:]
    rows, owned = hits.shape[1:]
    tile = tile_ref[...]

    @pl.when(pl.program_id(0) == 0)
    def _():
        for j in range(2):
            held = tile[:, 2 * j + 1 : 2 * j + 2].astype(i32)
            hit = jnp.where(held == iota((rows, owned), 1) + 1, 1.0, 0.0)
            hits[j] = hit.astype(bf16)
            turned[j] = hit.T.astype(bf16)

    cols = in_ref.shape[1] // 2
    gradient = None
    for j in range(2):
        values = decode(in_ref[:, j * cols : (j + 1) * cols], tile[:, 2 * j : 2 * j + 1])
        term = halves_dot(turned[j], values)
        gradient = term if gradient is None else gradient + term
    half = step(gradient, *refs[:6])
    for j in range(2):
        out_ref[:, j * cols : (j + 1) * cols] = jnp.dot(
            hits[j], half, preferred_element_type=f32
        ).astype(bf16)


def adam_b_kernel(me_ref, grad_ref, *refs):
    refs[-1][...] = step(grad_ref[...], *refs[:3], *refs[-4:-1])


def pick_kernel(owned, wb, me_ref, tile_ref, in_ref, out_ref, made, sems):
    rows = made.shape[0]
    shape = (rows, owned)
    hit = tile_ref[...][:, 2:3].astype(i32) == iota(shape, 1) + 1
    quarter = which(iota(shape, 0))
    picker = jnp.concatenate([ones(hit & (quarter == h)) for h in range(QUAD)], axis=1)
    sent = []
    for i in range(2):
        block = jnp.concatenate(
            [in_ref[(2 * h + i) * owned : (2 * h + i + 1) * owned] for h in range(QUAD)], axis=0
        )
        cut = pl.ds(i * wb, wb)
        made[:, cut] = jnp.dot(picker, block, preferred_element_type=f32).astype(bf16)
        sent.append(pltpu.make_async_copy(made.at[:, cut], out_ref.at[:, cut], sems.at[i]))
        sent[-1].start()
    for copy in sent:
        copy.wait()


def unpad_kernel(owned, me_ref, in_ref, *refs):
    names, outs = refs[: len(refs) // 2], refs[len(refs) // 2 :]
    rows = in_ref.shape[0]
    n, wa = outs[0].shape
    for j in range(len(outs) // QUAD):
        finder = []
        for t in range(QUAD):
            _, col, _ = positions(names[QUAD * j + t][:1, :n].astype(i32), owned)
            at = iota((n, rows), 1)
            finder.append(ones((place_of(at) == col) & (which(at) == t)))
        finder = jnp.concatenate(finder, axis=0)
        for c in range(wa // COLS):
            first = (2 * c + j) * COLS
            found = jnp.dot(
                finder, in_ref[:, first : first + COLS], preferred_element_type=f32
            ).astype(bf16)
            for t in range(QUAD):
                outs[QUAD * j + t][:, c * COLS : (c + 1) * COLS] = found[t * n : (t + 1) * n]


def final_kernel(owned, reps, width, wa, me_ref, ids_ref, in_ref, *refs):
    ins, out_ref, found, sems, sem_b = refs[:reps], refs[-4], refs[-3], refs[-2], refs[-1]
    r = me_ref[1]
    wb = width - wa
    n, rows = out_ref.shape[0], in_ref.shape[0]
    copies = []
    for s in range(reps):
        start = pl.multiple_of((r + s) % reps * width, LANES)
        copies.append(pltpu.make_async_copy(ins[s], out_ref.at[:, pl.ds(start, wa)], sems.at[s]))
        copies[-1].start()
    _, col, _ = positions(ids_ref[...], owned)
    at = iota((n, rows), 1)
    hit = place_of(at) == col
    finder = jnp.concatenate([ones(hit & (which(at) == h)) for h in range(QUAD)], axis=0)
    for i in range(2):
        rows_b = jnp.dot(
            finder, in_ref[:, i * wb : (i + 1) * wb], preferred_element_type=f32
        ).astype(bf16)
        for h in range(QUAD):
            s = 2 * h + i
            found[s] = rows_b[h * n : (h + 1) * n]
            cut = pl.ds(s * width + wa, wb)
            copies.append(pltpu.make_async_copy(found.at[s], out_ref.at[:, cut], sem_b.at[s]))
            copies[-1].start()
    for copy in copies:
        copy.wait()


def shards(token_grads, token_slots, touched_ids, table, first_moment, second_moment):
    owners, reps = lax.axis_size("vocab"), lax.axis_size("rep")
    tokens, full = token_grads.shape
    touched = touched_ids.shape[0]
    owned, width = table.shape
    wa = PART_A
    wb = width - wa
    rows = owners * QUAD * CAP
    slots = token_slots.reshape(1, tokens)
    ids = touched_ids.reshape(1, touched)
    me = jnp.stack([lax.axis_index("vocab"), lax.axis_index("rep")]).astype(i32)
    dma = pltpu.SemaphoreType.DMA

    def over_vocab(x):
        x = x.reshape(owners, QUAD * CAP, -1)
        return lax.all_to_all(x, "vocab", split_axis=0, concat_axis=0, tiled=True).reshape(rows, -1)

    def shift(x, s):
        if s == 0:
            return x
        return lax.ppermute(x, "rep", [(i, (i + s) % reps) for i in range(reps)])

    def together(*lists):
        done = lax.optimization_barrier(tuple(x for many in lists for x in many))
        starts = [sum(map(len, lists[:j])) for j in range(len(lists))]
        return [done[first : first + len(many)] for first, many in zip(starts, lists)]

    wide = touched // SUB * wa + LANES
    sums = call(
        functools.partial(sums_kernel, width),
        "sums",
        [sds((SUB, wide), i16)] * reps,
        (1,),
        [whole((1, tokens)), whole((1, touched)), ANY],
        [whole((SUB, wide))] * reps,
        2 * touched * tokens * wa * reps,
        (tokens + touched) * 2 * wa * reps,
        scratch=[pltpu.VMEM((reps, tokens, wa), bf16), dma((reps,))],
    )(me, slots, ids, token_grads)
    group = [shift(x, s) for s, x in enumerate(sums)]

    out_b = call(
        functools.partial(send_kernel, width, wa, owned),
        "send",
        sds((rows, 2 * wb + LANES), i16),
        (1,),
        [whole((1, tokens)), whole((1, touched)), ANY, ANY],
        ANY,
        16 * rows * tokens * wb,
        (tokens * reps + rows * 2) * 2 * wb,
        scratch=[
            pltpu.VMEM((reps, tokens, wb), bf16),
            pltpu.VMEM((rows, 2 * wb + LANES), i16),
            dma((reps,)),
            dma((3,)),
        ],
    )(me, slots, ids, sums[0], token_grads)
    arrived_b = over_vocab(out_b)
    tile_b = pl.BlockSpec((rows, LANES), lambda i, me: (0, 2 * wb // LANES))

    dense = call(
        functools.partial(place_kernel, owned, wb),
        "place",
        sds((reps * owned, wb), f32),
        (1,),
        [whole((rows, 2 * wb + LANES))],
        ANY,
        8 * rows * QUAD * owned * wb,
        (rows + owned * reps) * 4 * wb,
        scratch=[pltpu.VMEM((2, QUAD * owned, wb), f32), dma((reps,))],
    )(me, arrived_b)
    group, (dense,) = together(group, [dense])
    gradient_b = lax.psum_scatter(dense, "rep", scatter_dimension=0, tiled=True)

    steps_a = wa // COLS
    wide_a = 2 * wa + LANES
    out_a = call(
        functools.partial(route_kernel, owned, wa),
        "route",
        sds((rows, wide_a), i16),
        (1,),
        [whole((SUB, wide))] * reps,
        ANY,
        8 * rows * QUAD * touched * wa,
        (rows * 2 + reps * touched) * 2 * wa,
        scratch=[pltpu.VMEM((rows, wide_a), i16), dma((steps_a + 1,))],
    )(me, *group)
    arrived_a = over_vocab(out_a)

    spec = pl.BlockSpec((owned, COLS), lambda i, me: (0, i))
    pair = pl.BlockSpec((rows, 2 * COLS), lambda i, me: (0, i))
    *news, back_a = call(
        adam_a_kernel,
        "adam_a",
        [*(sds((owned, width), f32) for _ in range(3)), sds((rows, 2 * wa), bf16)],
        (steps_a,),
        [pl.BlockSpec((rows, LANES), lambda i, me: (0, 2 * wa // LANES)), pair, spec, spec, spec],
        [spec, spec, spec, pair],
        12 * rows * owned * wa,
        (rows * 8 + owned * 24) * wa,
        scratch=[pltpu.VMEM((2, rows, owned), bf16), pltpu.VMEM((2, owned, rows), bf16)],
    )(me, arrived_a, arrived_a, table, first_moment, second_moment)
    spec_b = pl.BlockSpec((owned, COLS_B), lambda i, me: (0, wa // COLS_B + i))
    spec_h = pl.BlockSpec((owned, COLS_B), lambda i, me: (0, i))
    *news, half_b = call(
        adam_b_kernel,
        "adam_b",
        [*(sds((owned, width), f32) for _ in range(3)), sds((owned, wb), bf16)],
        (wb // COLS_B,),
        [spec_h, spec_b, spec_b, spec_b, ANY, ANY, ANY],
        [spec_b, spec_b, spec_b, spec_h],
        20 * owned * wb,
        30 * owned * wb,
        aliases={5 + j: j for j in range(3)},
    )(me, gradient_b, table, first_moment, second_moment, *news)
    rows_b = lax.all_gather(half_b, "rep", axis=0, tiled=True)

    returned_a = over_vocab(back_a)

    mine_a = call(
        functools.partial(unpad_kernel, owned),
        "unpad",
        [sds((touched, wa), bf16)] * reps,
        (1,),
        [whole((rows, 2 * wa))]
        + [pl.BlockSpec((SUB, LANES), lambda i, me: (0, touched // SUB * wa // LANES))] * reps,
        [whole((touched, wa))] * reps,
        2 * reps * touched * rows * wa,
        (rows * 2 + reps * touched) * 2 * wa,
    )(me, returned_a, *group)
    home_a = [shift(x, (reps - s) % reps) for s, x in enumerate(mine_a)]
    first, (rows_b,) = together([home_a[s] for s in SOON], [rows_b])
    for s, x in zip(SOON, first):
        home_a[s] = x
    back_b = call(
        functools.partial(pick_kernel, owned, wb),
        "pick",
        sds((rows, 2 * wb), bf16),
        (1,),
        [tile_b, whole((reps * owned, wb))],
        ANY,
        4 * rows * QUAD * owned * wb,
        (reps * owned + 2 * rows) * wb * 2,
        scratch=[pltpu.VMEM((rows, 2 * wb), bf16), dma((2,))],
    )(me, arrived_b, rows_b)
    returned_b = over_vocab(back_b)

    refreshed = call(
        functools.partial(final_kernel, owned, reps, width, wa),
        "final",
        sds((touched, full), bf16),
        (1,),
        [whole((1, touched)), whole((rows, 2 * wb))] + [whole((touched, wa))] * reps,
        ANY,
        16 * touched * rows * wb,
        touched * full * 4,
        scratch=[pltpu.VMEM((reps, touched, wb), bf16), dma((reps,)), dma((reps,))],
    )(me, ids, returned_b, *home_a)
    return (*news, refreshed)


def solution(mesh):
    return jax.shard_map(
        shards,
        mesh=mesh,
        in_specs=(
            P(("vocab", "rep"), None),
            P(("vocab", "rep")),
            P(("vocab", "rep")),
            P("vocab", "rep"),
            P("vocab", "rep"),
            P("vocab", "rep"),
        ),
        out_specs=(
            P("vocab", "rep"),
            P("vocab", "rep"),
            P("vocab", "rep"),
            P(("vocab", "rep"), None),
        ),
        check_vma=False,
    )
```

```python
import functools
import math
import jax
import jax.numpy as jnp
from jax import lax
from jax.experimental import pallas as pl
from jax.experimental.pallas import tpu as pltpu
from jax.sharding import PartitionSpec as P

STEP = 4
decay_first = 0.9
decay_second = 0.95
learn_rate = 0.03
epsilon = 1e-08

CAP = 4
QUAD = 4
SUB, LANES = 16, 128
PART_A, COLS = 1152, 384
ORDER = (3, 5, 2, 6, 4, 1, 7)
SOON = (1, 7)
TOP = 32000.0
PER_OCTAVE = 64.0 / math.log(2.0)
f32, bf16, i32, i16 = jnp.float32, jnp.bfloat16, jnp.int32, jnp.int16
sds = jax.ShapeDtypeStruct
ANY = pl.BlockSpec(memory_space=pl.ANY)


def iota(shape, dim):
    return lax.broadcasted_iota(i32, shape, dim)


def ones(hit):
    return jnp.where(hit, 1.0, 0.0).astype(bf16)


def whole(shape):
    return pl.BlockSpec(shape, lambda *_: (0,) * len(shape))


def call(body, name, out_shape, grid, in_specs, out_specs, flops, nbytes, aliases=None, scratch=(), room=24):
    return pl.pallas_call(
        body,
        out_shape=out_shape,
        grid_spec=pltpu.PrefetchScalarGridSpec(
            num_scalar_prefetch=1,
            grid=grid,
            in_specs=in_specs,
            out_specs=out_specs,
            scratch_shapes=scratch,
        ),
        input_output_aliases=aliases or {},
        compiler_params=pltpu.CompilerParams(vmem_limit_bytes=room << 20),
        cost_estimate=pl.CostEstimate(flops=flops, bytes_accessed=nbytes, transcendentals=0),
        name=name,
    )


def to_i16(values):
    return values.astype(i32).astype(i16)


def to_f32(codes):
    return codes.astype(i32).astype(f32)


def encode(values):
    most = jnp.max(jnp.abs(values), axis=1, keepdims=True)
    level = jnp.ceil(jnp.log(jnp.maximum(most, 1e-30)) * PER_OCTAVE)
    return to_i16(jnp.round(values * (jnp.exp(level * (-1.0 / PER_OCTAVE)) * TOP))), level


def decode(codes, level):
    return to_f32(codes) * (jnp.exp(to_f32(level) * (1.0 / PER_OCTAVE)) * (1.0 / TOP))


def halves_dot(onehot, values):
    upper = values.astype(bf16)
    lower = (values - upper.astype(f32)).astype(bf16)
    return jnp.dot(onehot, upper, preferred_element_type=f32) + jnp.dot(
        onehot, lower, preferred_element_type=f32
    )


def codes_dot(onehot, codes):
    upper = jnp.floor(codes * (1.0 / 256.0))
    lower = codes - upper * 256.0
    return 256.0 * jnp.dot(onehot, upper.astype(bf16), preferred_element_type=f32) + jnp.dot(
        onehot, lower.astype(bf16), preferred_element_type=f32
    )


def positions(ids_row, owned):
    n = ids_row.shape[1]
    ids = jnp.broadcast_to(ids_row, (n, n))
    at, along = iota((n, n), 0), iota((n, n), 1)
    owner_row = ids // owned
    ids_col = jnp.sum(jnp.where(at == along, ids, 0), axis=1, keepdims=True)
    owner_col = jnp.broadcast_to(ids_col // owned, (n, n))
    same = owner_row == owner_col
    rank_row = jnp.sum(jnp.where(same & (at < along), 1, 0), axis=0, keepdims=True)
    rank_col = jnp.sum(jnp.where(same & (along < at), 1, 0), axis=1, keepdims=True)
    return owner_row[:1] * CAP + rank_row, owner_col[:, :1] * CAP + rank_col, ids_col


def place_of(at):
    return at // (QUAD * CAP) * CAP + at % CAP


def which(at):
    return at // CAP % QUAD


def load_columns(source, buf, sems, firsts):
    width = buf.shape[2]
    copies = [
        pltpu.make_async_copy(source.at[:, pl.ds(first, width)], buf.at[j], sems.at[j])
        for j, first in enumerate(firsts)
    ]
    for copy in copies:
        copy.start()
    return copies


def sums_kernel(width, me_ref, slots_ref, ids_ref, grads_ref, *refs):
    outs, (buf, sems) = refs[:-2], refs[-2:]
    reps, n, tokens, wa = len(outs), ids_ref.shape[1], slots_ref.shape[1], buf.shape[2]
    copies = load_columns(
        grads_ref,
        buf,
        sems,
        [pl.multiple_of((me_ref[1] + s) % reps * width, LANES) for s in range(reps)],
    )
    member = ones(jnp.broadcast_to(slots_ref[...], (n, tokens)) == iota((n, tokens), 0))
    lane = iota((SUB, LANES), 1)
    names = jnp.concatenate([jnp.broadcast_to(ids_ref[...], (SUB, n)), jnp.zeros((SUB, LANES - n), i32)], axis=1)
    for s in range(reps):
        copies[s].wait()
        codes, level = encode(jnp.dot(member, buf[s], preferred_element_type=f32))
        tile = names.astype(f32)
        for g in range(n // SUB):
            outs[s][:, g * wa : (g + 1) * wa] = codes[g * SUB : (g + 1) * SUB]
            tile = jnp.where(lane == n + g, level[g * SUB : (g + 1) * SUB], tile)
        outs[s][:, n // SUB * wa :] = to_i16(tile)


def send_kernel(width, wa, owned, me_ref, slots_ref, ids_ref, after_ref, grads_ref, out_ref, buf, made, sems, out_sems):
    reps, tokens, wb = buf.shape
    n, rows = ids_ref.shape[1], made.shape[0]
    copies = load_columns(
        grads_ref,
        buf,
        sems,
        [s * width + wa for s in range(reps)],
    )
    place_row, place_col, _ = positions(ids_ref[...], owned)
    slot = jnp.broadcast_to(slots_ref[...], (n, tokens))
    of_token = jnp.sum(
        jnp.where(slot == iota((n, tokens), 0), place_col, 0), axis=0, keepdims=True
    )
    at = iota((rows, tokens), 0)
    hit = place_of(at) == of_token
    member = jnp.concatenate([ones(hit & (which(at) == h)) for h in range(QUAD)], axis=1)
    local = ids_ref[...] % owned + 1
    held = jnp.sum(jnp.where(place_of(iota((rows, n), 0)) == place_row, local, 0), axis=1, keepdims=True)
    lane = iota((rows, LANES), 1)
    tile = jnp.where(lane == 2, held, 0).astype(f32)
    for copy in copies:
        copy.wait()
    sent = []
    for i in range(3):
        if i < 2:
            block = jnp.concatenate([buf[2 * h + i] for h in range(QUAD)], axis=0)
            codes, level = encode(jnp.dot(member, block, preferred_element_type=f32))
            tile = jnp.where(lane == i, level, tile)
            cut = pl.ds(i * wb, wb)
            made[:, cut] = codes
        else:
            cut = pl.ds(2 * wb, LANES)
            made[:, cut] = to_i16(tile)
        sent.append(pltpu.make_async_copy(made.at[:, cut], out_ref.at[:, cut], out_sems.at[i]))
        sent[-1].start()
    for copy in sent:
        copy.wait()


def route_kernel(owned, wa, me_ref, *refs):
    ins, (out_ref, made, sems) = refs[:-3], refs[-3:]
    rows = made.shape[0]
    groups = (ins[0].shape[1] - LANES) // wa
    n = groups * SUB
    lane = iota((rows, LANES), 1)
    tile = jnp.zeros((rows, LANES), f32)
    hits = []
    for j in range(len(ins) // QUAD):
        hot, extra = [], []
        for t in range(QUAD):
            last = ins[QUAD * j + t][:, groups * wa :].astype(i32)
            place_row, _, ids_col = positions(last[:1, :n], owned)
            at = iota((rows, n), 0)
            hot.append(ones((place_of(at) == place_row) & (which(at) == t)))
            level = jnp.concatenate([last[:, n + g : n + g + 1] for g in range(groups)], axis=0)
            pair = iota((n, LANES), 1)
            extra.append(
                jnp.where(pair == 2 * j, level, jnp.where(pair == 2 * j + 1, ids_col % owned + 1, 0)).astype(f32)
            )
        hits.append(jnp.concatenate(hot, axis=1))
        tile = tile + codes_dot(hits[j], jnp.concatenate(extra, axis=0))
    made[:, 2 * wa :] = to_i16(tile)
    sent = [pltpu.make_async_copy(made.at[:, pl.ds(2 * wa, LANES)], out_ref.at[:, pl.ds(2 * wa, LANES)], sems.at[0])]
    sent[-1].start()
    for c in range(wa // COLS):
        for j in range(len(hits)):
            codes = jnp.concatenate(
                [
                    to_f32(x[:, g * wa + c * COLS : g * wa + (c + 1) * COLS])
                    for x in ins[QUAD * j : QUAD * (j + 1)]
                    for g in range(groups)
                ],
                axis=0,
            )
            first = (2 * c + j) * COLS
            made[:, first : first + COLS] = to_i16(codes_dot(hits[j], codes))
        cut = pl.ds(2 * c * COLS, 2 * COLS)
        sent.append(pltpu.make_async_copy(made.at[:, cut], out_ref.at[:, cut], sems.at[c + 1]))
        sent[-1].start()
    for copy in sent:
        copy.wait()


def place_kernel(owned, wb, me_ref, in_ref, out_ref, made, sems):
    rows = in_ref.shape[0]
    tile = in_ref[:, 2 * wb :]
    held = tile[:, 2:3].astype(i32)
    shape = (rows, owned)
    hit = jnp.where(held == iota(shape, 1) + 1, 1.0, 0.0).T
    quarter = which(iota((owned, rows), 1))
    placer = jnp.concatenate(
        [jnp.where(quarter == h, hit, 0.0).astype(bf16) for h in range(QUAD)], axis=0
    )
    sent = []
    for i in range(2):
        values = decode(in_ref[:, i * wb : (i + 1) * wb], tile[:, i : i + 1])
        made[i] = halves_dot(placer, values)
        for h in range(QUAD):
            q = 2 * h + i
            sent.append(
                pltpu.make_async_copy(
                    made.at[i, pl.ds(h * owned, owned)], out_ref.at[pl.ds(q * owned, owned)], sems.at[q]
                )
            )
            sent[-1].start()
    for copy in sent:
        copy.wait()


def step(gradient, table_ref, first_ref, second_ref, new_table_ref, new_first_ref, new_second_ref):
    new_first = decay_first * first_ref[...] + (1.0 - decay_first) * gradient
    new_second = decay_second * second_ref[...] + (1.0 - decay_second) * gradient * gradient
    scaled_first = new_first / (1.0 - decay_first**STEP)
    scaled_second = new_second / (1.0 - decay_second**STEP)
    new_table = table_ref[...] - learn_rate * scaled_first / (jnp.sqrt(scaled_second) + epsilon)
    new_table_ref[...] = new_table
    new_first_ref[...] = new_first
    new_second_ref[...] = new_second
    return new_table.astype(bf16)


def adam_a_kernel(me_ref, tile_ref, in_ref, *refs):
    out_ref, hits, turned = refs[-3:]
    rows, owned = hits.shape[1:]
    tile = tile_ref[...]

    @pl.when(pl.program_id(0) == 0)
    def _():
        for j in range(2):
            held = tile[:, 2 * j + 1 : 2 * j + 2].astype(i32)
            hit = jnp.where(held == iota((rows, owned), 1) + 1, 1.0, 0.0)
            hits[j] = hit.astype(bf16)
            turned[j] = hit.T.astype(bf16)

    cols = in_ref.shape[1] // 2
    gradient = None
    for j in range(2):
        values = decode(in_ref[:, j * cols : (j + 1) * cols], tile[:, 2 * j : 2 * j + 1])
        term = halves_dot(turned[j], values)
        gradient = term if gradient is None else gradient + term
    half = step(gradient, *refs[:6])
    for j in range(2):
        out_ref[:, j * cols : (j + 1) * cols] = jnp.dot(
            hits[j], half, preferred_element_type=f32
        ).astype(bf16)


def adam_b_kernel(me_ref, grad_ref, *refs):
    refs[-1][...] = step(grad_ref[...], *refs[:3], *refs[-4:-1])


def pick_kernel(owned, wb, me_ref, tile_ref, in_ref, out_ref, made, sems):
    rows = made.shape[0]
    shape = (rows, owned)
    hit = tile_ref[...][:, 2:3].astype(i32) == iota(shape, 1) + 1
    quarter = which(iota(shape, 0))
    picker = jnp.concatenate([ones(hit & (quarter == h)) for h in range(QUAD)], axis=1)
    sent = []
    for i in range(2):
        block = jnp.concatenate(
            [in_ref[(2 * h + i) * owned : (2 * h + i + 1) * owned] for h in range(QUAD)], axis=0
        )
        cut = pl.ds(i * wb, wb)
        made[:, cut] = jnp.dot(picker, block, preferred_element_type=f32).astype(bf16)
        sent.append(pltpu.make_async_copy(made.at[:, cut], out_ref.at[:, cut], sems.at[i]))
        sent[-1].start()
    for copy in sent:
        copy.wait()


def unpad_kernel(owned, me_ref, in_ref, *refs):
    names, outs = refs[: len(refs) // 2], refs[len(refs) // 2 :]
    rows = in_ref.shape[0]
    n, wa = outs[0].shape
    for j in range(len(outs) // QUAD):
        finder = []
        for t in range(QUAD):
            _, col, _ = positions(names[QUAD * j + t][:1, :n].astype(i32), owned)
            at = iota((n, rows), 1)
            finder.append(ones((place_of(at) == col) & (which(at) == t)))
        finder = jnp.concatenate(finder, axis=0)
        for c in range(wa // COLS):
            first = (2 * c + j) * COLS
            found = jnp.dot(
                finder, in_ref[:, first : first + COLS], preferred_element_type=f32
            ).astype(bf16)
            for t in range(QUAD):
                outs[QUAD * j + t][:, c * COLS : (c + 1) * COLS] = found[t * n : (t + 1) * n]


def final_kernel(owned, reps, width, wa, me_ref, ids_ref, in_ref, *refs):
    ins, out_ref, found, sems, sem_b = refs[:reps], refs[-4], refs[-3], refs[-2], refs[-1]
    r = me_ref[1]
    wb = width - wa
    n, rows = out_ref.shape[0], in_ref.shape[0]
    copies = []
    for x, s in zip(ins, (*ORDER, 0)):
        start = pl.multiple_of((r + s) % reps * width, LANES)
        copies.append(pltpu.make_async_copy(x, out_ref.at[:, pl.ds(start, wa)], sems.at[s]))
        copies[-1].start()
    _, col, _ = positions(ids_ref[...], owned)
    at = iota((n, rows), 1)
    hit = place_of(at) == col
    finder = jnp.concatenate([ones(hit & (which(at) == h)) for h in range(QUAD)], axis=0)
    for i in range(2):
        rows_b = jnp.dot(
            finder, in_ref[:, i * wb : (i + 1) * wb], preferred_element_type=f32
        ).astype(bf16)
        for h in range(QUAD):
            s = 2 * h + i
            found[s] = rows_b[h * n : (h + 1) * n]
            cut = pl.ds(s * width + wa, wb)
            copies.append(pltpu.make_async_copy(found.at[s], out_ref.at[:, cut], sem_b.at[s]))
            copies[-1].start()
    for copy in copies:
        copy.wait()


def shards(token_grads, token_slots, touched_ids, table, first_moment, second_moment):
    owners, reps = lax.axis_size("vocab"), lax.axis_size("rep")
    tokens, full = token_grads.shape
    touched = touched_ids.shape[0]
    owned, width = table.shape
    wa = PART_A
    wb = width - wa
    rows = owners * QUAD * CAP
    slots = token_slots.reshape(1, tokens)
    ids = touched_ids.reshape(1, touched)
    me = jnp.stack([lax.axis_index("vocab"), lax.axis_index("rep")]).astype(i32)
    dma = pltpu.SemaphoreType.DMA

    def over_vocab(x):
        x = x.reshape(owners, QUAD * CAP, -1)
        return lax.all_to_all(x, "vocab", split_axis=0, concat_axis=0, tiled=True).reshape(rows, -1)

    def shift(x, s):
        if s == 0:
            return x
        return lax.ppermute(x, "rep", [(i, (i + s) % reps) for i in range(reps)])

    def together(*lists):
        done = lax.optimization_barrier(tuple(x for many in lists for x in many))
        starts = [sum(map(len, lists[:j])) for j in range(len(lists))]
        return [done[first : first + len(many)] for first, many in zip(starts, lists)]

    wide = touched // SUB * wa + LANES
    sums = call(
        functools.partial(sums_kernel, width),
        "sums",
        [sds((SUB, wide), i16)] * reps,
        (1,),
        [whole((1, tokens)), whole((1, touched)), ANY],
        [whole((SUB, wide))] * reps,
        2 * touched * tokens * wa * reps,
        (tokens + touched) * 2 * wa * reps,
        scratch=[pltpu.VMEM((reps, tokens, wa), bf16), dma((reps,))],
        room=56,
    )(me, slots, ids, token_grads)
    group = list(sums)
    for s in ORDER:
        group[s] = shift(sums[s], s)

    out_b = call(
        functools.partial(send_kernel, width, wa, owned),
        "send",
        sds((rows, 2 * wb + LANES), i16),
        (1,),
        [whole((1, tokens)), whole((1, touched)), ANY, ANY],
        ANY,
        16 * rows * tokens * wb,
        (tokens * reps + rows * 2) * 2 * wb,
        scratch=[
            pltpu.VMEM((reps, tokens, wb), bf16),
            pltpu.VMEM((rows, 2 * wb + LANES), i16),
            dma((reps,)),
            dma((3,)),
        ],
        room=56,
    )(me, slots, ids, sums[0], token_grads)
    arrived_b = over_vocab(out_b)
    tile_b = pl.BlockSpec((rows, LANES), lambda i, me: (0, 2 * wb // LANES))

    dense = call(
        functools.partial(place_kernel, owned, wb),
        "place",
        sds((reps * owned, wb), f32),
        (1,),
        [whole((rows, 2 * wb + LANES))],
        ANY,
        8 * rows * QUAD * owned * wb,
        (rows + owned * reps) * 4 * wb,
        scratch=[pltpu.VMEM((2, QUAD * owned, wb), f32), dma((reps,))],
        room=56,
    )(me, arrived_b)
    far, (dense,) = together([group[s] for s in ORDER], [dense])
    for s, x in zip(ORDER, far):
        group[s] = x
    gradient_b = lax.psum_scatter(dense, "rep", scatter_dimension=0, tiled=True)

    steps_a = wa // COLS
    wide_a = 2 * wa + LANES
    out_a = call(
        functools.partial(route_kernel, owned, wa),
        "route",
        sds((rows, wide_a), i16),
        (1,),
        [whole((SUB, wide))] * reps,
        ANY,
        8 * rows * QUAD * touched * wa,
        (rows * 2 + reps * touched) * 2 * wa,
        scratch=[pltpu.VMEM((rows, wide_a), i16), dma((steps_a + 1,))],
    )(me, *group)
    arrived_a = over_vocab(out_a)

    spec = pl.BlockSpec((owned, COLS), lambda i, me: (0, i))
    pair = pl.BlockSpec((rows, 2 * COLS), lambda i, me: (0, i))
    *news, back_a = call(
        adam_a_kernel,
        "adam_a",
        [*(sds((owned, width), f32) for _ in range(3)), sds((rows, 2 * wa), bf16)],
        (steps_a,),
        [pl.BlockSpec((rows, LANES), lambda i, me: (0, 2 * wa // LANES)), pair, spec, spec, spec],
        [spec, spec, spec, pair],
        12 * rows * owned * wa,
        (rows * 8 + owned * 24) * wa,
        scratch=[pltpu.VMEM((2, rows, owned), bf16), pltpu.VMEM((2, owned, rows), bf16)],
    )(me, arrived_a, arrived_a, table, first_moment, second_moment)
    spec_b = pl.BlockSpec((pl.Element(owned), pl.Element(wb)), lambda i, me: (0, wa))
    spec_h = whole((owned, wb))
    *news, half_b = call(
        adam_b_kernel,
        "adam_b",
        [*(sds((owned, width), f32) for _ in range(3)), sds((owned, wb), bf16)],
        (1,),
        [spec_h, spec_b, spec_b, spec_b, ANY, ANY, ANY],
        [spec_b, spec_b, spec_b, spec_h],
        20 * owned * wb,
        30 * owned * wb,
        aliases={5 + j: j for j in range(3)},
        room=56,
    )(me, gradient_b, table, first_moment, second_moment, *news)
    rows_b = lax.all_gather(half_b, "rep", axis=0, tiled=True)

    returned_a = over_vocab(back_a)

    mine_a = call(
        functools.partial(unpad_kernel, owned),
        "unpad",
        [sds((touched, wa), bf16)] * reps,
        (1,),
        [whole((rows, 2 * wa))]
        + [pl.BlockSpec((SUB, LANES), lambda i, me: (0, touched // SUB * wa // LANES))] * reps,
        [whole((touched, wa))] * reps,
        2 * reps * touched * rows * wa,
        (rows * 2 + reps * touched) * 2 * wa,
    )(me, returned_a, *group)
    home_a = list(mine_a)
    for s in ORDER:
        home_a[s] = shift(mine_a[s], reps - s)
    first, (rows_b,) = together([home_a[s] for s in SOON], [rows_b])
    for s, x in zip(SOON, first):
        home_a[s] = x
    back_b = call(
        functools.partial(pick_kernel, owned, wb),
        "pick",
        sds((rows, 2 * wb), bf16),
        (1,),
        [tile_b, whole((reps * owned, wb))],
        ANY,
        4 * rows * QUAD * owned * wb,
        (reps * owned + 2 * rows) * wb * 2,
        scratch=[pltpu.VMEM((rows, 2 * wb), bf16), dma((2,))],
    )(me, arrived_b, rows_b)
    returned_b = over_vocab(back_b)

    refreshed = call(
        functools.partial(final_kernel, owned, reps, width, wa),
        "final",
        sds((touched, full), bf16),
        (1,),
        [whole((1, touched)), whole((rows, 2 * wb))] + [whole((touched, wa))] * reps,
        ANY,
        16 * touched * rows * wb,
        touched * full * 4,
        scratch=[pltpu.VMEM((reps, touched, wb), bf16), dma((reps,)), dma((reps,))],
    )(me, ids, returned_b, *[home_a[s] for s in (*ORDER, 0)])
    return (*news, refreshed)


def solution(mesh):
    return jax.shard_map(
        shards,
        mesh=mesh,
        in_specs=(
            P(("vocab", "rep"), None),
            P(("vocab", "rep")),
            P(("vocab", "rep")),
            P("vocab", "rep"),
            P("vocab", "rep"),
            P("vocab", "rep"),
        ),
        out_specs=(
            P("vocab", "rep"),
            P("vocab", "rep"),
            P("vocab", "rep"),
            P(("vocab", "rep"), None),
        ),
        check_vma=False,
    )
```

```python
import functools
import math
import jax
import jax.numpy as jnp
from jax import lax
from jax.experimental import pallas as pl
from jax.experimental.pallas import tpu as pltpu
from jax.sharding import PartitionSpec as P

STEP = 4
decay_first = 0.9
decay_second = 0.95
learn_rate = 0.03
epsilon = 1e-08

CAP = 4
QUAD = 4
SUB, LANES = 16, 128
PART_A, COLS = 1152, 384
ORDER = (4, 3, 5, 2, 6, 1, 7)
SOON = (1, 7)
TOP = 32000.0
PER_OCTAVE = 64.0 / math.log(2.0)
f32, bf16, i32, i16 = jnp.float32, jnp.bfloat16, jnp.int32, jnp.int16
sds = jax.ShapeDtypeStruct
ANY = pl.BlockSpec(memory_space=pl.ANY)


def iota(shape, dim):
    return lax.broadcasted_iota(i32, shape, dim)


def ones(hit):
    return jnp.where(hit, 1.0, 0.0).astype(bf16)


def whole(shape):
    return pl.BlockSpec(shape, lambda *_: (0,) * len(shape))


def call(body, name, out_shape, grid, in_specs, out_specs, flops, nbytes, aliases=None, scratch=(), room=24):
    return pl.pallas_call(
        body,
        out_shape=out_shape,
        grid_spec=pltpu.PrefetchScalarGridSpec(
            num_scalar_prefetch=1,
            grid=grid,
            in_specs=in_specs,
            out_specs=out_specs,
            scratch_shapes=scratch,
        ),
        input_output_aliases=aliases or {},
        compiler_params=pltpu.CompilerParams(vmem_limit_bytes=room << 20),
        cost_estimate=pl.CostEstimate(flops=flops, bytes_accessed=nbytes, transcendentals=0),
        name=name,
    )


def to_i16(values):
    return values.astype(i32).astype(i16)


def to_f32(codes):
    return codes.astype(i32).astype(f32)


def encode(values):
    most = jnp.max(jnp.abs(values), axis=1, keepdims=True)
    level = jnp.ceil(jnp.log(jnp.maximum(most, 1e-30)) * PER_OCTAVE)
    return to_i16(jnp.round(values * (jnp.exp(level * (-1.0 / PER_OCTAVE)) * TOP))), level


def decode(codes, level):
    return to_f32(codes) * (jnp.exp(to_f32(level) * (1.0 / PER_OCTAVE)) * (1.0 / TOP))


def halves_dot(onehot, values):
    upper = values.astype(bf16)
    lower = (values - upper.astype(f32)).astype(bf16)
    return jnp.dot(onehot, upper, preferred_element_type=f32) + jnp.dot(
        onehot, lower, preferred_element_type=f32
    )


def codes_dot(onehot, codes):
    upper = jnp.floor(codes * (1.0 / 256.0))
    lower = codes - upper * 256.0
    return 256.0 * jnp.dot(onehot, upper.astype(bf16), preferred_element_type=f32) + jnp.dot(
        onehot, lower.astype(bf16), preferred_element_type=f32
    )


def positions(ids_row, owned):
    n = ids_row.shape[1]
    ids = jnp.broadcast_to(ids_row, (n, n))
    at, along = iota((n, n), 0), iota((n, n), 1)
    owner_row = ids // owned
    ids_col = jnp.sum(jnp.where(at == along, ids, 0), axis=1, keepdims=True)
    owner_col = jnp.broadcast_to(ids_col // owned, (n, n))
    same = owner_row == owner_col
    rank_row = jnp.sum(jnp.where(same & (at < along), 1, 0), axis=0, keepdims=True)
    rank_col = jnp.sum(jnp.where(same & (along < at), 1, 0), axis=1, keepdims=True)
    return owner_row[:1] * CAP + rank_row, owner_col[:, :1] * CAP + rank_col, ids_col


def place_of(at):
    return at // (QUAD * CAP) * CAP + at % CAP


def which(at):
    return at // CAP % QUAD


def load_columns(source, buf, sems, firsts):
    width = buf.shape[2]
    copies = [
        pltpu.make_async_copy(source.at[:, pl.ds(first, width)], buf.at[j], sems.at[j])
        for j, first in enumerate(firsts)
    ]
    for copy in copies:
        copy.start()
    return copies


def sums_kernel(width, me_ref, slots_ref, ids_ref, grads_ref, *refs):
    outs, (buf, sems) = refs[:-2], refs[-2:]
    reps, n, tokens, wa = len(outs), ids_ref.shape[1], slots_ref.shape[1], buf.shape[2]
    copies = load_columns(
        grads_ref,
        buf,
        sems,
        [pl.multiple_of((me_ref[1] + s) % reps * width, LANES) for s in range(reps)],
    )
    member = ones(jnp.broadcast_to(slots_ref[...], (n, tokens)) == iota((n, tokens), 0))
    lane = iota((SUB, LANES), 1)
    names = jnp.concatenate([jnp.broadcast_to(ids_ref[...], (SUB, n)), jnp.zeros((SUB, LANES - n), i32)], axis=1)
    for s in range(reps):
        copies[s].wait()
        codes, level = encode(jnp.dot(member, buf[s], preferred_element_type=f32))
        tile = names.astype(f32)
        for g in range(n // SUB):
            outs[s][:, g * wa : (g + 1) * wa] = codes[g * SUB : (g + 1) * SUB]
            tile = jnp.where(lane == n + g, level[g * SUB : (g + 1) * SUB], tile)
        outs[s][:, n // SUB * wa :] = to_i16(tile)


def send_kernel(width, wa, owned, me_ref, slots_ref, ids_ref, after_ref, grads_ref, out_ref, buf, made, sems, out_sems):
    reps, tokens, wb = buf.shape
    n, rows = ids_ref.shape[1], made.shape[0]
    copies = load_columns(
        grads_ref,
        buf,
        sems,
        [s * width + wa for s in range(reps)],
    )
    place_row, place_col, _ = positions(ids_ref[...], owned)
    slot = jnp.broadcast_to(slots_ref[...], (n, tokens))
    of_token = jnp.sum(
        jnp.where(slot == iota((n, tokens), 0), place_col, 0), axis=0, keepdims=True
    )
    at = iota((rows, tokens), 0)
    hit = place_of(at) == of_token
    member = jnp.concatenate([ones(hit & (which(at) == h)) for h in range(QUAD)], axis=1)
    local = ids_ref[...] % owned + 1
    held = jnp.sum(jnp.where(place_of(iota((rows, n), 0)) == place_row, local, 0), axis=1, keepdims=True)
    lane = iota((rows, LANES), 1)
    tile = jnp.where(lane == 2, held, 0).astype(f32)
    for copy in copies:
        copy.wait()
    sent = []
    for i in range(3):
        if i < 2:
            block = jnp.concatenate([buf[2 * h + i] for h in range(QUAD)], axis=0)
            codes, level = encode(jnp.dot(member, block, preferred_element_type=f32))
            tile = jnp.where(lane == i, level, tile)
            cut = pl.ds(i * wb, wb)
            made[:, cut] = codes
        else:
            cut = pl.ds(2 * wb, LANES)
            made[:, cut] = to_i16(tile)
        sent.append(pltpu.make_async_copy(made.at[:, cut], out_ref.at[:, cut], out_sems.at[i]))
        sent[-1].start()
    for copy in sent:
        copy.wait()


def route_kernel(owned, wa, me_ref, *refs):
    ins, (out_ref, made, sems) = refs[:-3], refs[-3:]
    rows = made.shape[0]
    groups = (ins[0].shape[1] - LANES) // wa
    n = groups * SUB
    lane = iota((rows, LANES), 1)
    tile = jnp.zeros((rows, LANES), f32)
    hits = []
    for j in range(len(ins) // QUAD):
        hot, extra = [], []
        for t in range(QUAD):
            last = ins[QUAD * j + t][:, groups * wa :].astype(i32)
            place_row, _, ids_col = positions(last[:1, :n], owned)
            at = iota((rows, n), 0)
            hot.append(ones((place_of(at) == place_row) & (which(at) == t)))
            level = jnp.concatenate([last[:, n + g : n + g + 1] for g in range(groups)], axis=0)
            pair = iota((n, LANES), 1)
            extra.append(
                jnp.where(pair == 2 * j, level, jnp.where(pair == 2 * j + 1, ids_col % owned + 1, 0)).astype(f32)
            )
        hits.append(jnp.concatenate(hot, axis=1))
        tile = tile + codes_dot(hits[j], jnp.concatenate(extra, axis=0))
    made[:, 2 * wa :] = to_i16(tile)
    sent = [pltpu.make_async_copy(made.at[:, pl.ds(2 * wa, LANES)], out_ref.at[:, pl.ds(2 * wa, LANES)], sems.at[0])]
    sent[-1].start()
    for c in range(wa // COLS):
        for j in range(len(hits)):
            codes = jnp.concatenate(
                [
                    to_f32(x[:, g * wa + c * COLS : g * wa + (c + 1) * COLS])
                    for x in ins[QUAD * j : QUAD * (j + 1)]
                    for g in range(groups)
                ],
                axis=0,
            )
            first = (2 * c + j) * COLS
            made[:, first : first + COLS] = to_i16(codes_dot(hits[j], codes))
        cut = pl.ds(2 * c * COLS, 2 * COLS)
        sent.append(pltpu.make_async_copy(made.at[:, cut], out_ref.at[:, cut], sems.at[c + 1]))
        sent[-1].start()
    for copy in sent:
        copy.wait()


def place_kernel(owned, wb, me_ref, in_ref, out_ref, made, sems):
    rows = in_ref.shape[0]
    tile = in_ref[:, 2 * wb :]
    held = tile[:, 2:3].astype(i32)
    shape = (rows, owned)
    hit = jnp.where(held == iota(shape, 1) + 1, 1.0, 0.0).T
    quarter = which(iota((owned, rows), 1))
    placer = jnp.concatenate(
        [jnp.where(quarter == h, hit, 0.0).astype(bf16) for h in range(QUAD)], axis=0
    )
    sent = []
    for i in range(2):
        values = decode(in_ref[:, i * wb : (i + 1) * wb], tile[:, i : i + 1])
        made[i] = halves_dot(placer, values)
        for h in range(QUAD):
            q = 2 * h + i
            sent.append(
                pltpu.make_async_copy(
                    made.at[i, pl.ds(h * owned, owned)], out_ref.at[pl.ds(q * owned, owned)], sems.at[q]
                )
            )
            sent[-1].start()
    for copy in sent:
        copy.wait()


def step(gradient, table_ref, first_ref, second_ref, new_table_ref, new_first_ref, new_second_ref):
    new_first = decay_first * first_ref[...] + (1.0 - decay_first) * gradient
    new_second = decay_second * second_ref[...] + (1.0 - decay_second) * gradient * gradient
    scaled_first = new_first / (1.0 - decay_first**STEP)
    scaled_second = new_second / (1.0 - decay_second**STEP)
    new_table = table_ref[...] - learn_rate * scaled_first / (jnp.sqrt(scaled_second) + epsilon)
    new_table_ref[...] = new_table
    new_first_ref[...] = new_first
    new_second_ref[...] = new_second
    return new_table.astype(bf16)


def adam_a_kernel(me_ref, tile_ref, in_ref, *refs):
    out_ref, hits, turned = refs[-3:]
    rows, owned = hits.shape[1:]
    tile = tile_ref[...]

    @pl.when(pl.program_id(0) == 0)
    def _():
        for j in range(2):
            held = tile[:, 2 * j + 1 : 2 * j + 2].astype(i32)
            hit = jnp.where(held == iota((rows, owned), 1) + 1, 1.0, 0.0)
            hits[j] = hit.astype(bf16)
            turned[j] = hit.T.astype(bf16)

    cols = in_ref.shape[1] // 2
    gradient = None
    for j in range(2):
        values = decode(in_ref[:, j * cols : (j + 1) * cols], tile[:, 2 * j : 2 * j + 1])
        term = halves_dot(turned[j], values)
        gradient = term if gradient is None else gradient + term
    half = step(gradient, *refs[:6])
    for j in range(2):
        out_ref[:, j * cols : (j + 1) * cols] = jnp.dot(
            hits[j], half, preferred_element_type=f32
        ).astype(bf16)


def adam_b_kernel(me_ref, grad_ref, *refs):
    refs[-1][...] = step(grad_ref[...], *refs[:3], *refs[-4:-1])


def pick_kernel(owned, wb, me_ref, tile_ref, in_ref, out_ref, made, sems):
    rows = made.shape[0]
    shape = (rows, owned)
    hit = tile_ref[...][:, 2:3].astype(i32) == iota(shape, 1) + 1
    quarter = which(iota(shape, 0))
    picker = jnp.concatenate([ones(hit & (quarter == h)) for h in range(QUAD)], axis=1)
    sent = []
    for i in range(2):
        block = jnp.concatenate(
            [in_ref[(2 * h + i) * owned : (2 * h + i + 1) * owned] for h in range(QUAD)], axis=0
        )
        cut = pl.ds(i * wb, wb)
        made[:, cut] = jnp.dot(picker, block, preferred_element_type=f32).astype(bf16)
        sent.append(pltpu.make_async_copy(made.at[:, cut], out_ref.at[:, cut], sems.at[i]))
        sent[-1].start()
    for copy in sent:
        copy.wait()


def unpad_kernel(owned, me_ref, in_ref, *refs):
    names, outs = refs[: len(refs) // 2], refs[len(refs) // 2 :]
    rows = in_ref.shape[0]
    n, wa = outs[0].shape
    for j in range(len(outs) // QUAD):
        finder = []
        for t in range(QUAD):
            _, col, _ = positions(names[QUAD * j + t][:1, :n].astype(i32), owned)
            at = iota((n, rows), 1)
            finder.append(ones((place_of(at) == col) & (which(at) == t)))
        finder = jnp.concatenate(finder, axis=0)
        for c in range(wa // COLS):
            first = (2 * c + j) * COLS
            found = jnp.dot(
                finder, in_ref[:, first : first + COLS], preferred_element_type=f32
            ).astype(bf16)
            for t in range(QUAD):
                outs[QUAD * j + t][:, c * COLS : (c + 1) * COLS] = found[t * n : (t + 1) * n]


def final_kernel(owned, reps, width, wa, me_ref, ids_ref, in_ref, *refs):
    ins, out_ref, found, sems, sem_b = refs[:reps], refs[-4], refs[-3], refs[-2], refs[-1]
    r = me_ref[1]
    wb = width - wa
    n, rows = out_ref.shape[0], in_ref.shape[0]
    copies = []
    for x, s in zip(ins, (*ORDER, 0)):
        start = pl.multiple_of((r + s) % reps * width, LANES)
        copies.append(pltpu.make_async_copy(x, out_ref.at[:, pl.ds(start, wa)], sems.at[s]))
        copies[-1].start()
    _, col, _ = positions(ids_ref[...], owned)
    at = iota((n, rows), 1)
    hit = place_of(at) == col
    finder = jnp.concatenate([ones(hit & (which(at) == h)) for h in range(QUAD)], axis=0)
    for i in range(2):
        rows_b = jnp.dot(
            finder, in_ref[:, i * wb : (i + 1) * wb], preferred_element_type=f32
        ).astype(bf16)
        for h in range(QUAD):
            s = 2 * h + i
            found[s] = rows_b[h * n : (h + 1) * n]
            cut = pl.ds(s * width + wa, wb)
            copies.append(pltpu.make_async_copy(found.at[s], out_ref.at[:, cut], sem_b.at[s]))
            copies[-1].start()
    for copy in copies:
        copy.wait()


def shards(token_grads, token_slots, touched_ids, table, first_moment, second_moment):
    owners, reps = lax.axis_size("vocab"), lax.axis_size("rep")
    tokens, full = token_grads.shape
    touched = touched_ids.shape[0]
    owned, width = table.shape
    wa = PART_A
    wb = width - wa
    rows = owners * QUAD * CAP
    slots = token_slots.reshape(1, tokens)
    ids = touched_ids.reshape(1, touched)
    me = jnp.stack([lax.axis_index("vocab"), lax.axis_index("rep")]).astype(i32)
    dma = pltpu.SemaphoreType.DMA

    def over_vocab(x):
        x = x.reshape(owners, QUAD * CAP, -1)
        return lax.all_to_all(x, "vocab", split_axis=0, concat_axis=0, tiled=True).reshape(rows, -1)

    def shift(x, s):
        if s == 0:
            return x
        return lax.ppermute(x, "rep", [(i, (i + s) % reps) for i in range(reps)])

    def together(*lists):
        done = lax.optimization_barrier(tuple(x for many in lists for x in many))
        starts = [sum(map(len, lists[:j])) for j in range(len(lists))]
        return [done[first : first + len(many)] for first, many in zip(starts, lists)]

    wide = touched // SUB * wa + LANES
    sums = call(
        functools.partial(sums_kernel, width),
        "sums",
        [sds((SUB, wide), i16)] * reps,
        (1,),
        [whole((1, tokens)), whole((1, touched)), ANY],
        [whole((SUB, wide))] * reps,
        2 * touched * tokens * wa * reps,
        (tokens + touched) * 2 * wa * reps,
        scratch=[pltpu.VMEM((reps, tokens, wa), bf16), dma((reps,))],
        room=56,
    )(me, slots, ids, token_grads)
    group = list(sums)
    for s in ORDER:
        group[s] = shift(sums[s], s)

    out_b = call(
        functools.partial(send_kernel, width, wa, owned),
        "send",
        sds((rows, 2 * wb + LANES), i16),
        (1,),
        [whole((1, tokens)), whole((1, touched)), ANY, ANY],
        ANY,
        16 * rows * tokens * wb,
        (tokens * reps + rows * 2) * 2 * wb,
        scratch=[
            pltpu.VMEM((reps, tokens, wb), bf16),
            pltpu.VMEM((rows, 2 * wb + LANES), i16),
            dma((reps,)),
            dma((3,)),
        ],
        room=56,
    )(me, slots, ids, sums[0], token_grads)
    arrived_b = over_vocab(out_b)
    tile_b = pl.BlockSpec((rows, LANES), lambda i, me: (0, 2 * wb // LANES))

    dense = call(
        functools.partial(place_kernel, owned, wb),
        "place",
        sds((reps * owned, wb), f32),
        (1,),
        [whole((rows, 2 * wb + LANES))],
        ANY,
        8 * rows * QUAD * owned * wb,
        (rows + owned * reps) * 4 * wb,
        scratch=[pltpu.VMEM((2, QUAD * owned, wb), f32), dma((reps,))],
        room=56,
    )(me, arrived_b)
    far, (dense,) = together([group[s] for s in ORDER], [dense])
    for s, x in zip(ORDER, far):
        group[s] = x
    gradient_b = lax.psum_scatter(dense, "rep", scatter_dimension=0, tiled=True)

    steps_a = wa // COLS
    wide_a = 2 * wa + LANES
    out_a = call(
        functools.partial(route_kernel, owned, wa),
        "route",
        sds((rows, wide_a), i16),
        (1,),
        [whole((SUB, wide))] * reps,
        ANY,
        8 * rows * QUAD * touched * wa,
        (rows * 2 + reps * touched) * 2 * wa,
        scratch=[pltpu.VMEM((rows, wide_a), i16), dma((steps_a + 1,))],
    )(me, *group)
    arrived_a = over_vocab(out_a)

    spec = pl.BlockSpec((owned, COLS), lambda i, me: (0, i))
    pair = pl.BlockSpec((rows, 2 * COLS), lambda i, me: (0, i))
    *news, back_a = call(
        adam_a_kernel,
        "adam_a",
        [*(sds((owned, width), f32) for _ in range(3)), sds((rows, 2 * wa), bf16)],
        (steps_a,),
        [pl.BlockSpec((rows, LANES), lambda i, me: (0, 2 * wa // LANES)), pair, spec, spec, spec],
        [spec, spec, spec, pair],
        12 * rows * owned * wa,
        (rows * 8 + owned * 24) * wa,
        scratch=[pltpu.VMEM((2, rows, owned), bf16), pltpu.VMEM((2, owned, rows), bf16)],
    )(me, arrived_a, arrived_a, table, first_moment, second_moment)
    spec_b = pl.BlockSpec((pl.Element(owned), pl.Element(wb)), lambda i, me: (0, wa))
    spec_h = whole((owned, wb))
    *news, half_b = call(
        adam_b_kernel,
        "adam_b",
        [*(sds((owned, width), f32) for _ in range(3)), sds((owned, wb), bf16)],
        (1,),
        [spec_h, spec_b, spec_b, spec_b, ANY, ANY, ANY],
        [spec_b, spec_b, spec_b, spec_h],
        20 * owned * wb,
        30 * owned * wb,
        aliases={5 + j: j for j in range(3)},
        room=56,
    )(me, gradient_b, table, first_moment, second_moment, *news)
    rows_b = lax.all_gather(half_b, "rep", axis=0, tiled=True)

    returned_a = over_vocab(back_a)

    mine_a = call(
        functools.partial(unpad_kernel, owned),
        "unpad",
        [sds((touched, wa), bf16)] * reps,
        (1,),
        [whole((rows, 2 * wa))]
        + [pl.BlockSpec((SUB, LANES), lambda i, me: (0, touched // SUB * wa // LANES))] * reps,
        [whole((touched, wa))] * reps,
        2 * reps * touched * rows * wa,
        (rows * 2 + reps * touched) * 2 * wa,
    )(me, returned_a, *group)
    home_a = list(mine_a)
    for s in ORDER:
        home_a[s] = shift(mine_a[s], reps - s)
    first, (rows_b,) = together([home_a[s] for s in SOON], [rows_b])
    for s, x in zip(SOON, first):
        home_a[s] = x
    back_b = call(
        functools.partial(pick_kernel, owned, wb),
        "pick",
        sds((rows, 2 * wb), bf16),
        (1,),
        [tile_b, whole((reps * owned, wb))],
        ANY,
        4 * rows * QUAD * owned * wb,
        (reps * owned + 2 * rows) * wb * 2,
        scratch=[pltpu.VMEM((rows, 2 * wb), bf16), dma((2,))],
    )(me, arrived_b, rows_b)
    returned_b = over_vocab(back_b)

    refreshed = call(
        functools.partial(final_kernel, owned, reps, width, wa),
        "final",
        sds((touched, full), bf16),
        (1,),
        [whole((1, touched)), whole((rows, 2 * wb))] + [whole((touched, wa))] * reps,
        ANY,
        16 * touched * rows * wb,
        touched * full * 4,
        scratch=[pltpu.VMEM((reps, touched, wb), bf16), dma((reps,)), dma((reps,))],
    )(me, ids, returned_b, *[home_a[s] for s in (*ORDER, 0)])
    return (*news, refreshed)


def solution(mesh):
    return jax.shard_map(
        shards,
        mesh=mesh,
        in_specs=(
            P(("vocab", "rep"), None),
            P(("vocab", "rep")),
            P(("vocab", "rep")),
            P("vocab", "rep"),
            P("vocab", "rep"),
            P("vocab", "rep"),
        ),
        out_specs=(
            P("vocab", "rep"),
            P("vocab", "rep"),
            P("vocab", "rep"),
            P(("vocab", "rep"), None),
        ),
        check_vma=False,
    )
```
